128 devices in a mesh: replica: 2 (over z_hi), fsdp: 64 (over x, z_lo, y, core).
Axes of the slice: x: 4, y: 4, z: 4 (z_hi: 2, z_lo: 2; z = z_hi * 2 + z_lo), core: 2. Of those that a mesh axis runs over, the one named last changes fastest.
Arguments:
- inputs: bfloat16 [2, 4096, 2048], P('replica', 'fsdp'), may hold values from -6 to 6
- cotangent: bfloat16 [2, 4096, 2048], P('replica', 'fsdp'), may hold values from -0.0014648438 to 0.0014648438
- params_in: float32 [2, 2, 2048, 8192], P('replica', None, None, 'fsdp'), may hold values from -0.125 to 0.125
- params_down: float32 [2, 8192, 2048], P('replica', 'fsdp'), may hold values from -0.0625 to 0.0625
- first_in: bfloat16 [2, 2, 2048, 8192], P('replica', None, None, 'fsdp'), may hold values from -0.017944336 to 0.017944336
- first_down: bfloat16 [2, 8192, 2048], P('replica', 'fsdp'), may hold values from -0.017944336 to 0.017944336
- second_in: bfloat16 [2, 2, 2048, 8192], P('replica', None, None, 'fsdp'), may hold values from 9.983778e-07 to 9.9658966e-05
- second_down: bfloat16 [2, 8192, 2048], P('replica', 'fsdp'), may hold values from 9.983778e-07 to 9.9658966e-05
- base_in: float32 [2, 2048, 8192], P(None, None, 'fsdp'), may hold values from -0.125 to 0.125
- base_down: float32 [8192, 2048], P('fsdp'), may hold values from -0.0625 to 0.0625
- outer_in: float32 [2, 2048, 8192], P(None, None, 'fsdp'), may hold values from -0.06 to 0.06
- outer_down: float32 [8192, 2048], P('fsdp'), may hold values from -0.06 to 0.06
Outputs:
- new_base_in: float32 [2, 2048, 8192], P(None, None, 'fsdp')
- new_base_down: float32 [8192, 2048], P('fsdp')
- new_outer_in: float32 [2, 2048, 8192], P(None, None, 'fsdp')
- new_outer_down: float32 [8192, 2048], P('fsdp')
- new_first_in: bfloat16 [2, 2, 2048, 8192], P('replica', None, None, 'fsdp')
- new_first_down: bfloat16 [2, 8192, 2048], P('replica', 'fsdp')
- new_second_in: bfloat16 [2, 2, 2048, 8192], P('replica', None, None, 'fsdp')
- new_second_down: bfloat16 [2, 8192, 2048], P('replica', 'fsdp')
The draws below stay inside these ranges and needn't reach their ends.
All inputs are finite; a program needn't handle non-finite values.
Results may differ from the reference program's by a relative error of at most 0.0055.
Values may be sent and summed in bfloat16 or wider, within the bound.
No kernel may reach another device: no remote copies, remote signals or barrier semaphores. Data moves between devices by JAX's collectives and lax.ppermute only.
A program may use at most 128 MiB of HBM per device.

```python
import math
import jax
import jax.numpy as jnp
from jax import lax

D = 2048
FF = 8192
TOK_DEV = 64
TOKENS = 4096
REPLICAS = 2
N_FSDP = 64


def block_levels(rng, shape, shards, smallest, top_value):
    level, own = 1.0, jax.random.fold_in(rng, 6)
    for dim, shards_of in shards:
        heights = jnp.exp(jax.random.uniform(jax.random.fold_in(own, dim), (shards_of,), jnp.float32, smallest / len(shards), top_value / len(shards)))
        level = level * jnp.repeat(heights, shape[dim] // shards_of).reshape([-1 if axis == dim else 1 for axis in range(len(shape))])
    return level


def gaussian(own_key, dims, deviation, most, shards=(), kind=jnp.bfloat16):
    array = deviation * jax.random.normal(own_key, dims, jnp.float32)
    if shards:
        array = array * block_levels(own_key, dims, shards, -0.22, 0.18)
    return jnp.clip(array, -most, most).astype(kind)


def setup_inputs(seed: int = 0) -> dict:
    streams_of = jax.random.split(jax.random.key(seed), 13)
    return {
        "inputs": gaussian(streams_of[0], (REPLICAS, TOKENS, D), 1.0, 6.0, ((0, 2), (1, 64))),
        "cotangent": gaussian(streams_of[1], (REPLICAS, TOKENS, D), (1.0 / (TOK_DEV * N_FSDP)), 0.0014648438, ((0, 2), (1, 64))),
        "params_in": gaussian(streams_of[2], (REPLICAS, 2, D, FF), D ** -0.5, 0.125, ((0, 2), (3, 64)), jnp.float32),
        "params_down": gaussian(streams_of[3], (REPLICAS, FF, D), FF ** -0.5, 0.0625, ((0, 2), (1, 64)), jnp.float32),
        "first_in": gaussian(streams_of[4], (REPLICAS, 2, D, FF), 0.003, 0.017944336, ((0, 2), (3, 64))),
        "first_down": gaussian(streams_of[5], (REPLICAS, FF, D), 0.003, 0.017944336, ((0, 2), (1, 64))),
        "second_in": jnp.clip(jnp.exp(math.log(9.965896606445312e-05) - 4.6033775 * jax.random.uniform(streams_of[6], (REPLICAS, 2, D, FF), jnp.float32) ** block_levels(streams_of[6], (REPLICAS, 2, D, FF), ((0, 2), (3, 64)), -0.2, 0.2)), 9.98377799987793e-07, 9.965896606445312e-05).astype(jnp.bfloat16),
        "second_down": jnp.clip(jnp.exp(math.log(9.965896606445312e-05) - 4.6033775 * jax.random.uniform(streams_of[7], (REPLICAS, FF, D), jnp.float32) ** block_levels(streams_of[7], (REPLICAS, FF, D), ((0, 2), (1, 64)), -0.2, 0.2)), 9.98377799987793e-07, 9.965896606445312e-05).astype(jnp.bfloat16),
        "base_in": gaussian(streams_of[8], (2, D, FF), D ** -0.5, 0.125, ((2, 64),), jnp.float32),
        "base_down": gaussian(streams_of[9], (FF, D), FF ** -0.5, 0.0625, ((0, 64),), jnp.float32),
        "outer_in": gaussian(streams_of[10], (2, D, FF), 0.01, 0.06, ((2, 64),), jnp.float32),
        "outer_down": gaussian(streams_of[11], (FF, D), 0.01, 0.06, ((0, 64),), jnp.float32),
    }


beta_one = 0.9
beta_two = 0.95
bias_one = 1.0 - 0.9 ** 64
bias_two = 1.0 - 0.95 ** 64
inner_rate = 0.004
decay_rate = 0.1
epsilon_adam = 1e-08
momentum_keep = 0.9
outer_rate = 0.7

def contract_rows(left, right):
    return lax.dot_general(left, right, (((0,), (0,)), ((), ())), preferred_element_type=jnp.float32)

def group_grads(rows_in, rows_cot, weights_in, weights_down):
    gate_w = weights_in[0].astype(jnp.bfloat16)
    up_w = weights_in[1].astype(jnp.bfloat16)
    down_w = weights_down.astype(jnp.bfloat16)
    gate_pre = jnp.dot(rows_in, gate_w, preferred_element_type=jnp.float32)
    up_proj = jnp.dot(rows_in, up_w, preferred_element_type=jnp.float32)
    sigmoid_gate = jax.nn.sigmoid(gate_pre)
    silu_gate = gate_pre * sigmoid_gate
    hidden = (silu_gate * up_proj).astype(jnp.bfloat16)
    grad_down = contract_rows(hidden, rows_cot)
    dhidden = lax.dot_general(rows_cot, down_w, (((1,), (1,)), ((), ())), preferred_element_type=jnp.float32)
    dgate = (dhidden * up_proj * (sigmoid_gate * (1.0 + gate_pre * (1.0 - sigmoid_gate)))).astype(jnp.bfloat16)
    dup = (dhidden * silu_gate).astype(jnp.bfloat16)
    grad_in = jnp.stack([contract_rows(rows_in, dgate), contract_rows(rows_in, dup)])
    return (grad_in, grad_down)

def adamw(param, grad, first, second):
    first_new = beta_one * first.astype(jnp.float32) + (1.0 - beta_one) * grad
    second_new = beta_two * second.astype(jnp.float32) + (1.0 - beta_two) * grad * grad
    update = first_new / bias_one / (jnp.sqrt(second_new / bias_two) + epsilon_adam)
    param_new = param - inner_rate * (update + decay_rate * param)
    return (param_new, first_new.astype(jnp.bfloat16), second_new.astype(jnp.bfloat16))

def reference(inputs, cotangent, params_in, params_down, first_in, first_down, second_in, second_down, base_in, base_down, outer_in, outer_down):
    total_in = jnp.zeros(base_in.shape, jnp.float32)
    total_down = jnp.zeros(base_down.shape, jnp.float32)
    firsts_in, firsts_down, seconds_in, seconds_down = ([], [], [], [])
    for member in range(REPLICAS):
        grad_in, grad_down = group_grads(inputs[member], cotangent[member], params_in[member], params_down[member])
        new_in, fin, sin = adamw(params_in[member], grad_in, first_in[member], second_in[member])
        new_down, fdown, sdown = adamw(params_down[member], grad_down, first_down[member], second_down[member])
        total_in = total_in + (base_in - new_in)
        total_down = total_down + (base_down - new_down)
        firsts_in.append(fin)
        firsts_down.append(fdown)
        seconds_in.append(sin)
        seconds_down.append(sdown)
    grad_outer_in = total_in / REPLICAS
    grad_outer_down = total_down / REPLICAS
    new_outer_in = momentum_keep * outer_in + grad_outer_in
    new_outer_down = momentum_keep * outer_down + grad_outer_down
    new_base_in = base_in - outer_rate * (grad_outer_in + momentum_keep * new_outer_in)
    new_base_down = base_down - outer_rate * (grad_outer_down + momentum_keep * new_outer_down)
    return (new_base_in, new_base_down, new_outer_in, new_outer_down, jnp.stack(firsts_in), jnp.stack(firsts_down), jnp.stack(seconds_in), jnp.stack(seconds_down))
```

```python
import functools

import jax
import jax.numpy as jnp
from jax import lax
from jax.experimental import pallas as pl
from jax.experimental.pallas import tpu as pltpu
from jax.sharding import PartitionSpec as P

beta_one = 0.9
beta_two = 0.95
bias_one = 1.0 - 0.9**64
bias_two = 1.0 - 0.95**64
inner_rate = 0.004
decay_rate = 0.1
epsilon_adam = 1e-08
momentum_keep = 0.9
outer_rate = 0.7

AXES = {"x": (4, 16), "z": (2, 8), "y": (4, 2), "core": (2, 1)}
FSDP = 64


def shift(value, axis, by):
    size, stride = AXES[axis]
    pairs = []
    for i in range(FSDP):
        place = (i // stride) % size
        pairs.append((i, i + ((place + by) % size - place) * stride))
    return lax.ppermute(value, "fsdp", pairs)


def after(values, *others):
    out = lax.optimization_barrier((values, others))
    return out[0]


def direct_ring(rows, axis):
    return [rows, shift(rows, axis, 1), shift(rows, axis, -1), shift(rows, axis, 2)]


def forward_kernel(count, *refs):
    gate_ref, up_ref, down_ref = refs[:3]
    pieces = refs[3 : 3 + 2 * count]
    outs = refs[3 + 2 * count :]
    for k in range(count):
        x_ref, c_ref = pieces[2 * k], pieces[2 * k + 1]
        rows_in, rows_cot = x_ref[0], c_ref[0]
        gate_pre = jnp.dot(rows_in, gate_ref[...], preferred_element_type=jnp.float32)
        up_proj = jnp.dot(rows_in, up_ref[...], preferred_element_type=jnp.float32)
        dhidden = lax.dot_general(
            rows_cot, down_ref[...], (((1,), (1,)), ((), ())), preferred_element_type=jnp.float32
        )
        sig = 1.0 / (1.0 + jnp.exp(-gate_pre))
        silu = gate_pre * sig
        outs[3 * k][...] = (silu * up_proj).astype(jnp.bfloat16)
        outs[3 * k + 1][...] = (dhidden * up_proj * (sig * (1.0 + gate_pre * (1.0 - sig)))).astype(
            jnp.bfloat16
        )
        outs[3 * k + 2][...] = (dhidden * silu).astype(jnp.bfloat16)


def plane(array, index):
    rows, width = array.shape[1:]
    return pl.BlockSpec((1, rows, width), lambda i, index=index: (index, 0, 0))


def forward(weights, pieces):
    gate_w, up_w, down_w = weights
    width = down_w.shape[0]
    operands, specs, shapes, out_specs = [], [], [], []
    for x, xi, c, ci in pieces:
        operands += [x, c]
        specs += [plane(x, xi), plane(c, ci)]
        rows = x.shape[1]
        shapes += [jax.ShapeDtypeStruct((rows, width), jnp.bfloat16)] * 3
        out_specs += [pl.BlockSpec((rows, width), lambda i: (0, 0))] * 3
    whole = [pl.BlockSpec(w.shape, lambda i: (0, 0)) for w in weights]
    total = sum(p[0].shape[1] for p in pieces)
    outs = pl.pallas_call(
        functools.partial(forward_kernel, len(pieces)),
        grid=(1,),
        in_specs=whole + specs,
        out_specs=out_specs,
        out_shape=shapes,
        cost_estimate=pl.CostEstimate(
            flops=2 * total * 2048 * 3 * width,
            bytes_accessed=total * 2048 * 4,
            transcendentals=total * width,
        ),
        compiler_params=pltpu.CompilerParams(vmem_limit_bytes=40 * 1024 * 1024),
        name="forward",
    )(gate_w, up_w, down_w, *operands)
    return [tuple(outs[3 * k : 3 * k + 3]) for k in range(len(pieces))]


def contract(left, right):
    return lax.dot_general(
        left, right, (((0,), (0,)), ((), ())), preferred_element_type=jnp.float32
    )


def grad_down_kernel(count, *refs):
    hidden, cot = refs[:count], refs[count : 2 * count]
    own_ref, send_ref = refs[2 * count :]
    half = own_ref.shape[0]
    total = contract(hidden[0][...], cot[0][0])
    for k in range(1, count):
        total += contract(hidden[k][...], cot[k][0])
    own_ref[...] = total[:half]
    send_ref[...] = total[half:].astype(jnp.bfloat16)


def grad_in_kernel(count, *refs):
    dgate, dup, rows = refs[:count], refs[count : 2 * count], refs[2 * count : 3 * count]
    own_ref, send_ref = refs[3 * count :]
    half = own_ref.shape[2]
    for which, grads in enumerate((dgate, dup)):
        total = contract(grads[0][...], rows[0][0])
        for k in range(1, count):
            total += contract(grads[k][...], rows[k][0])
        total = total.T
        own_ref[which] = total[:, :half]
        send_ref[which] = total[:, half:].astype(jnp.bfloat16)


TILE = 256


def column(array, index):
    return pl.BlockSpec((1, array.shape[1], TILE), lambda i, index=index: (index, 0, i))


def gradient_down(hidden, cots):
    width = hidden[0].shape[1]
    depth = cots[0][0].shape[2]
    half = width // 2
    return pl.pallas_call(
        functools.partial(grad_down_kernel, len(hidden)),
        grid=(depth // TILE,),
        in_specs=[pl.BlockSpec(h.shape, lambda i: (0, 0)) for h in hidden]
        + [column(c, k) for c, k in cots],
        out_specs=[pl.BlockSpec((half, TILE), lambda i: (0, i))] * 2,
        out_shape=[
            jax.ShapeDtypeStruct((half, depth), jnp.float32),
            jax.ShapeDtypeStruct((half, depth), jnp.bfloat16),
        ],
        compiler_params=pltpu.CompilerParams(vmem_limit_bytes=40 * 1024 * 1024),
        name="grad_down",
    )(*hidden, *[c for c, _ in cots])


def gradient_in(dgate, dup, rows):
    width = dgate[0].shape[1]
    depth = rows[0][0].shape[2]
    half = width // 2
    return pl.pallas_call(
        functools.partial(grad_in_kernel, len(dgate)),
        grid=(depth // TILE,),
        in_specs=[pl.BlockSpec(h.shape, lambda i: (0, 0)) for h in dgate + dup]
        + [column(c, k) for c, k in rows],
        out_specs=[pl.BlockSpec((2, TILE, half), lambda i: (0, i, 0))] * 2,
        out_shape=[
            jax.ShapeDtypeStruct((2, depth, half), jnp.float32),
            jax.ShapeDtypeStruct((2, depth, half), jnp.bfloat16),
        ],
        compiler_params=pltpu.CompilerParams(vmem_limit_bytes=40 * 1024 * 1024),
        name="grad_in",
    )(*dgate, *dup, *[c for c, _ in rows])


def adamw(param, grad, first, second):
    first_new = beta_one * first.astype(jnp.float32) + (1.0 - beta_one) * grad
    second_new = beta_two * second.astype(jnp.float32) + (1.0 - beta_two) * grad * grad
    update = first_new / bias_one / (jnp.sqrt(second_new / bias_two) + epsilon_adam)
    param_new = param - inner_rate * (update + decay_rate * param)
    return (param_new, first_new.astype(jnp.bfloat16), second_new.astype(jnp.bfloat16))


def outer_step(own, other, base, outer):
    grad_outer = (own.astype(jnp.float32) + other.astype(jnp.float32)) / 2.0
    new_outer = momentum_keep * outer + grad_outer
    new_base = base - outer_rate * (grad_outer + momentum_keep * new_outer)
    return (new_base, new_outer)


def local(
    inputs,
    cotangent,
    params_in,
    params_down,
    first_in,
    first_down,
    second_in,
    second_down,
    base_in,
    base_down,
    outer_in,
    outer_down,
):
    half = inputs.shape[1] // 2
    own = [
        jnp.concatenate([inputs[:, k * half : (k + 1) * half], cotangent[:, k * half : (k + 1) * half]])
        for k in range(2)
    ]
    routes = (("x", "y"), ("y", "x"))
    first_wave = [direct_ring(own[k], routes[k][0]) for k in range(2)]
    across = [shift(own[k], "z", 1) for k in range(2)]

    weights_own = [
        params_in[0, 0].astype(jnp.bfloat16),
        params_in[0, 1].astype(jnp.bfloat16),
        params_down[0].astype(jnp.bfloat16),
    ]
    gate_w, up_w, down_w = weights_own
    gate_o, up_o, down_o = [shift(w, "core", 1) for w in weights_own]
    weights = (
        jnp.concatenate([gate_w, gate_o], axis=1),
        jnp.concatenate([up_w, up_o], axis=1),
        jnp.concatenate([down_w, down_o], axis=0),
    )

    def gathered(ring):
        return jnp.concatenate(ring, axis=1)

    wave_one = [gathered(r) for r in first_wave]
    near_one = [
        (shift(wave_one[k], routes[k][1], 1), shift(wave_one[k], routes[k][1], -1)) for k in range(2)
    ]
    second_wave = [direct_ring(across[k], routes[k][0]) for k in range(2)]
    wave_two = [gathered(r) for r in second_wave]
    near_two = [
        (shift(wave_two[k], routes[k][1], 1), shift(wave_two[k], routes[k][1], -1)) for k in range(2)
    ]
    near_one = lax.optimization_barrier(near_one)

    def far(near):
        return [
            (shift(near[k][0][:1], routes[k][1], 1), shift(near[k][1][1:], routes[k][1], -1))
            for k in range(2)
        ]

    far_one = far(near_one)
    near_two = lax.optimization_barrier(near_two)
    far_two = far(near_two)

    groups = []
    for wave, near, distant in ((wave_one, near_one, far_one), (wave_two, near_two, far_two)):
        groups.append([(wave[k], 0, wave[k], 1) for k in range(2)])
        groups.append([(piece, 0, piece, 1) for k in range(2) for piece in near[k]])
        groups.append([(distant[k][0], 0, distant[k][1], 0) for k in range(2)])
    pieces = [piece for group in groups for piece in group]
    results = [r for group in groups for r in forward(weights, group)]

    own_down, send_down = gradient_down([r[0] for r in results], [(p[2], p[3]) for p in pieces])
    grad_down = own_down + shift(send_down, "core", 1).astype(jnp.float32)
    new_down, fdown, sdown = adamw(params_down[0], grad_down, first_down[0], second_down[0])
    delta_down = (base_down - new_down).astype(jnp.bfloat16)
    other_down = lax.ppermute(delta_down, "replica", [(0, 1), (1, 0)])

    own_in, send_in = gradient_in(
        [r[1] for r in results], [r[2] for r in results], [(p[0], p[1]) for p in pieces]
    )
    grad_in = own_in + shift(send_in, "core", 1).astype(jnp.float32)
    new_in, fin, sin = adamw(params_in[0], grad_in, first_in[0], second_in[0])
    delta_in = (base_in - new_in).astype(jnp.bfloat16)
    other_in = lax.ppermute(delta_in, "replica", [(0, 1), (1, 0)])

    new_base_down, new_outer_down = outer_step(delta_down, other_down, base_down, outer_down)
    new_base_in, new_outer_in = outer_step(delta_in, other_in, base_in, outer_in)
    return (
        new_base_in,
        new_base_down,
        new_outer_in,
        new_outer_down,
        fin[None],
        fdown[None],
        sin[None],
        sdown[None],
    )


def solution(mesh):
    in_specs = (
        P("replica", "fsdp", None),
        P("replica", "fsdp", None),
        P("replica", None, None, "fsdp"),
        P("replica", "fsdp", None),
        P("replica", None, None, "fsdp"),
        P("replica", "fsdp", None),
        P("replica", None, None, "fsdp"),
        P("replica", "fsdp", None),
        P(None, None, "fsdp"),
        P("fsdp", None),
        P(None, None, "fsdp"),
        P("fsdp", None),
    )
    out_specs = (
        P(None, None, "fsdp"),
        P("fsdp", None),
        P(None, None, "fsdp"),
        P("fsdp", None),
        P("replica", None, None, "fsdp"),
        P("replica", "fsdp", None),
        P("replica", None, None, "fsdp"),
        P("replica", "fsdp", None),
    )
    return jax.shard_map(local, mesh=mesh, in_specs=in_specs, out_specs=out_specs, check_vma=False)
```

```python
import functools

import jax
import jax.numpy as jnp
from jax import lax
from jax.experimental import pallas as pl
from jax.experimental.pallas import tpu as pltpu
from jax.sharding import PartitionSpec as P

beta_one = 0.9
beta_two = 0.95
bias_one = 1.0 - 0.9**64
bias_two = 1.0 - 0.95**64
inner_rate = 0.004
decay_rate = 0.1
epsilon_adam = 1e-08
momentum_keep = 0.9
outer_rate = 0.7

AXES = {"x": (4, 16), "z": (2, 8), "y": (4, 2), "core": (2, 1)}
FSDP = 64
BF16 = jnp.bfloat16
F32 = jnp.float32
VMEM = pl.BlockSpec(memory_space=pltpu.VMEM)
PARAMS = pltpu.CompilerParams(vmem_limit_bytes=12 * 1024 * 1024)


def move(value, axis, target):
    size, stride = AXES[axis]
    pairs = []
    for i in range(FSDP):
        place = (i // stride) % size
        pairs.append((i, i + (target(place) - place) * stride))
    return lax.ppermute(value, "fsdp", pairs)


def up_y(value):
    return move(value, "y", lambda p: (p + 1) % 4)


def down_y(value):
    return move(value, "y", lambda p: (p + 3) % 4)


def swap_z(value):
    return move(value, "z", lambda p: 1 - p)


def swap_core(value):
    return move(value, "core", lambda p: 1 - p)


def far_x(value):
    return move(value, "x", lambda p: (p + 2) % 4)


def near_x(value):
    return move(value, "x", lambda p: p ^ 1)


def swap_replica(value):
    return lax.ppermute(value, "replica", [(0, 1), (1, 0)])


def struct(shape, dtype):
    return jax.ShapeDtypeStruct(shape, dtype)


def weights_kernel(in_ref, down_ref, out_ref):
    out_ref[0] = in_ref[0, 0].astype(BF16).T
    out_ref[1] = in_ref[0, 1].astype(BF16).T
    out_ref[2] = down_ref[0].astype(BF16)


def own_weights(params_in, params_down):
    depth, width = params_in.shape[2:]
    return pl.pallas_call(
        weights_kernel,
        in_specs=[VMEM] * 2,
        out_specs=VMEM,
        out_shape=struct((3, width, depth), BF16),
        cost_estimate=pl.CostEstimate(
            flops=depth * width * 3, bytes_accessed=depth * width * 18, transcendentals=0
        ),
        compiler_params=PARAMS,
        name="own_weights",
    )(params_in, params_down)


def forward_kernel(planes, in_ref, down_ref, *refs):
    count = len(planes)
    pieces, outs = refs[: 2 * count], refs[2 * count :]
    hidden_ref, dgate_ref, dup_ref, rows_ref, cots_ref = outs
    start = 0
    for k, (x_plane, c_plane) in enumerate(planes):
        rows = pieces[2 * k].shape[1]
        rows_ref[start : start + rows] = pieces[2 * k][x_plane]
        cots_ref[start : start + rows] = pieces[2 * k + 1][c_plane]
        start += rows
    width = down_ref.shape[0]
    sides = (((1,), (1,)), ((), ()))
    both = lax.dot_general(in_ref[...], rows_ref[...], sides, preferred_element_type=F32)
    dhidden = lax.dot_general(down_ref[...], cots_ref[...], sides, preferred_element_type=F32)
    gate_pre, up_proj = both[:width], both[width:]
    sig = 1.0 / (1.0 + jnp.exp(-gate_pre))
    silu = gate_pre * sig
    hidden_ref[...] = (silu * up_proj).astype(BF16)
    dgate_ref[...] = (dhidden * up_proj * (sig * (1.0 + gate_pre * (1.0 - sig)))).astype(BF16)
    dup_ref[...] = (dhidden * silu).astype(BF16)


def forward(weights_in, weights_down, pieces):
    width, depth = weights_down.shape
    total = sum(p[0].shape[1] for p in pieces)
    operands = [a for x, _, c, _ in pieces for a in (x, c)]
    return pl.pallas_call(
        functools.partial(forward_kernel, [(p[1], p[3]) for p in pieces]),
        in_specs=[VMEM] * (2 + len(operands)),
        out_specs=[VMEM] * 5,
        out_shape=[struct((width, total), BF16)] * 3 + [struct((total, depth), BF16)] * 2,
        cost_estimate=pl.CostEstimate(
            flops=2 * total * depth * 3 * width,
            bytes_accessed=total * depth * 8 + 6 * width * depth,
            transcendentals=total * width,
        ),
        compiler_params=PARAMS,
        name="forward",
    )(weights_in, weights_down, *operands)


def gradient_kernel(count, *refs):
    left, right = refs[:count], refs[count : 2 * count]
    own_ref, near_ref, send_ref, all_ref = refs[2 * count :]
    quarter, depth = own_ref.shape
    start = 0
    for piece in left:
        all_ref[:, start : start + piece.shape[1]] = piece[...]
        start += piece.shape[1]
    tile = 256
    for i in range(depth // tile):
        at = slice(i * tile, (i + 1) * tile)
        columns = jnp.concatenate([piece[:, at] for piece in right], axis=0)
        total = jnp.dot(all_ref[...], columns, preferred_element_type=F32)
        own_ref[:, at] = total[:quarter]
        send_ref[0, :, at] = total[quarter : 2 * quarter].astype(BF16)
        near_ref[:, at] = total[2 * quarter : 3 * quarter]
        send_ref[1, :, at] = total[3 * quarter :].astype(BF16)


def gradient(left, right):
    width = left[0].shape[0]
    depth = right[0].shape[1]
    rows = sum(r.shape[0] for r in right)
    quarter = width // 4
    return pl.pallas_call(
        functools.partial(gradient_kernel, len(left)),
        in_specs=[VMEM] * (2 * len(left)),
        out_specs=[VMEM] * 3,
        out_shape=[
            struct((quarter, depth), F32),
            struct((quarter, depth), F32),
            struct((2, quarter, depth), BF16),
        ],
        scratch_shapes=[pltpu.VMEM((width, rows), BF16)],
        cost_estimate=pl.CostEstimate(
            flops=2 * rows * depth * width,
            bytes_accessed=rows * depth * 2 + rows * width * 2 + width * depth * 3,
            transcendentals=0,
        ),
        compiler_params=PARAMS,
        name="gradient",
    )(*left, *right)


def adamw(param, grad, first, second):
    first_new = beta_one * first.astype(F32) + (1.0 - beta_one) * grad
    second_new = beta_two * second.astype(F32) + (1.0 - beta_two) * grad * grad
    update = first_new / bias_one / (jnp.sqrt(second_new / bias_two) + epsilon_adam)
    param_new = param - inner_rate * (update + decay_rate * param)
    return (param_new, first_new.astype(BF16), second_new.astype(BF16))


def inner_kernel(which, *refs):
    own, core, near, param, first, second, base = refs[:7]
    first_out, second_out, delta_out = refs[-3:]
    at = pl.ds(pl.multiple_of(pl.program_id(0) * TILE, TILE), TILE)
    grad = own[:, at] + core[0, :, at].astype(F32) + near[:, at].astype(F32)
    if which is None:
        place, shared = (0, slice(None), at), (slice(None), at)
    else:
        grad = grad.T
        place, shared = (0, which, at), (which, at)
    new, first_new, second_new = adamw(param[place], grad, first[place], second[place])
    first_out[...] = first_new.reshape(first_out.shape)
    second_out[...] = second_new.reshape(second_out.shape)
    delta_out[...] = (base[shared] - new).astype(BF16)


TILE = 512


def inner_step(own, core, near, param, first, second, base, which=None, earlier=()):
    quarter, depth = own.shape
    if which is not None:
        state = pl.BlockSpec((1, 1, TILE, quarter), lambda i: (0, which, i, 0))
        delta = pl.BlockSpec((TILE, quarter), lambda i: (i, 0))
        delta_shape = (depth, quarter)
    else:
        state = pl.BlockSpec((1, quarter, TILE), lambda i: (0, 0, i))
        delta = pl.BlockSpec((quarter, TILE), lambda i: (0, i))
        delta_shape = (quarter, depth)
    return pl.pallas_call(
        functools.partial(inner_kernel, which),
        grid=(depth // TILE,),
        in_specs=[VMEM] * 7 + [pl.BlockSpec(memory_space=pl.ANY)] * len(earlier),
        out_specs=[state, state, delta],
        out_shape=[struct(first.shape, BF16), struct(second.shape, BF16), struct(delta_shape, BF16)],
        input_output_aliases={7 + k: k for k in range(len(earlier))},
        cost_estimate=pl.CostEstimate(
            flops=20 * quarter * depth, bytes_accessed=26 * quarter * depth, transcendentals=quarter * depth
        ),
        compiler_params=PARAMS,
        name="inner_step",
    )(own, core, near, param, first, second, base, *earlier)


def outer_kernel(which, *refs):
    own, other, base, outer = refs[:4]
    base_out, outer_out = refs[-2:]
    at = pl.ds(pl.multiple_of(pl.program_id(0) * TILE, TILE), TILE)
    if which is None:
        part = shared = (slice(None), at)
    else:
        part, shared = (at,), (which, at)
    grad = (own[part].astype(F32) + other[part].astype(F32)) / 2.0
    new_outer = momentum_keep * outer[shared] + grad
    outer_out[...] = new_outer.reshape(outer_out.shape)
    base_out[...] = (base[shared] - outer_rate * (grad + momentum_keep * new_outer)).reshape(base_out.shape)


def outer_step(own, other, base, outer, which=None, earlier=()):
    if which is not None:
        depth, quarter = own.shape
        shared = pl.BlockSpec((1, TILE, quarter), lambda i: (which, i, 0))
    else:
        quarter, depth = own.shape
        shared = pl.BlockSpec((quarter, TILE), lambda i: (0, i))
    return pl.pallas_call(
        functools.partial(outer_kernel, which),
        grid=(depth // TILE,),
        in_specs=[VMEM] * 4 + [pl.BlockSpec(memory_space=pl.ANY)] * len(earlier),
        out_specs=[shared, shared],
        out_shape=[struct(base.shape, F32), struct(outer.shape, F32)],
        input_output_aliases={4 + k: k for k in range(len(earlier))},
        cost_estimate=pl.CostEstimate(
            flops=8 * quarter * depth, bytes_accessed=20 * quarter * depth, transcendentals=0
        ),
        compiler_params=PARAMS,
        name="outer_step",
    )(own, other, base, outer, *earlier)


def after(value, *others):
    return lax.optimization_barrier((value, others))[0]


def y_ring(rows):
    low, high = up_y(rows), down_y(rows)
    return low, high, up_y(low[:1]), down_y(high[1:])


def local(
    inputs,
    cotangent,
    params_in,
    params_down,
    first_in,
    first_down,
    second_in,
    second_down,
    base_in,
    base_down,
    outer_in,
    outer_down,
):
    own = jnp.concatenate([inputs, cotangent])
    by_x = far_x(own)
    by_z = swap_z(own)
    low_own, high_own, far_own_x, far_own_c = y_ring(own)
    mine = own_weights(params_in, params_down)
    core = swap_core(mine)
    near = near_x(mine)
    both = swap_core(near)
    low_x, high_x, far_x_x, far_x_c = y_ring(by_x)
    by_xz = swap_z(by_x)
    low_z, high_z, far_z_x, far_z_c = y_ring(after(by_z, by_xz))
    low_xz, high_xz = swap_z(low_x), swap_z(high_x)
    far_xz_x, far_xz_c = up_y(low_xz[:1]), down_y(high_xz[1:])

    weights_in = jnp.concatenate([w[k] for k in range(2) for w in (mine, core, near, both)])
    weights_down = jnp.concatenate([w[2] for w in (mine, core, near, both)])

    def full(piece):
        return (piece, 0, piece, 1)

    def parted(x_piece, c_piece):
        return (x_piece, 0, c_piece, 0)

    groups = [
        [full(own), full(low_own), full(high_own), parted(far_own_x, far_own_c)],
        [full(by_x), full(low_x), full(high_x), parted(far_x_x, far_x_c)],
        [full(by_z), full(low_z), full(high_z), full(by_xz)],
        [parted(far_z_x, far_z_c), full(low_xz), full(high_xz), parted(far_xz_x, far_xz_c)],
    ]
    results = [forward(weights_in, weights_down, group) for group in groups]
    hidden, dgate, dup, rows, cots = [list(r) for r in zip(*results)]

    def summed(left, right):
        own_part, near_part, send = gradient(left, right)
        core_part = swap_core(send)
        near_part = near_x((near_part + core_part[1].astype(F32)).astype(BF16))
        return own_part, core_part, near_part

    sums_down = summed(hidden, cots)
    sums_gate = summed(dgate, rows)
    sums_up = summed(after(dup, sums_down[1]), rows)
    fdown, sdown, delta_down = inner_step(
        *sums_down, params_down, first_down, second_down, base_down
    )
    other_down = swap_replica(delta_down)
    fin, sin, delta_gate = inner_step(
        *sums_gate, params_in, first_in, second_in, base_in, which=0
    )
    other_gate = swap_replica(delta_gate)
    fin, sin, delta_up = inner_step(
        *sums_up, params_in, first_in, second_in, base_in, which=1, earlier=(fin, sin)
    )
    other_up = swap_replica(delta_up)

    new_base_down, new_outer_down = outer_step(delta_down, other_down, base_down, outer_down)
    new_in = outer_step(delta_gate, other_gate, base_in, outer_in, which=0)
    new_base_in, new_outer_in = outer_step(
        delta_up, other_up, base_in, outer_in, which=1, earlier=new_in
    )
    return (new_base_in, new_base_down, new_outer_in, new_outer_down, fin, fdown, sin, sdown)


def solution(mesh):
    in_specs = (
        P("replica", "fsdp", None),
        P("replica", "fsdp", None),
        P("replica", None, None, "fsdp"),
        P("replica", "fsdp", None),
        P("replica", None, None, "fsdp"),
        P("replica", "fsdp", None),
        P("replica", None, None, "fsdp"),
        P("replica", "fsdp", None),
        P(None, None, "fsdp"),
        P("fsdp", None),
        P(None, None, "fsdp"),
        P("fsdp", None),
    )
    out_specs = (
        P(None, None, "fsdp"),
        P("fsdp", None),
        P(None, None, "fsdp"),
        P("fsdp", None),
        P("replica", None, None, "fsdp"),
        P("replica", "fsdp", None),
        P("replica", None, None, "fsdp"),
        P("replica", "fsdp", None),
    )
    return jax.shard_map(local, mesh=mesh, in_specs=in_specs, out_specs=out_specs, check_vma=False)
```

```python
import functools

import jax
import jax.numpy as jnp
from jax import lax
from jax.experimental import pallas as pl
from jax.experimental.pallas import tpu as pltpu
from jax.sharding import PartitionSpec as P

beta_one = 0.9
beta_two = 0.95
bias_one = 1.0 - 0.9**64
bias_two = 1.0 - 0.95**64
inner_rate = 0.004
decay_rate = 0.1
epsilon_adam = 1e-08
momentum_keep = 0.9
outer_rate = 0.7

AXES = {"x": (4, 16), "z": (2, 8), "y": (4, 2), "core": (2, 1)}
FSDP = 64
BF16 = jnp.bfloat16
F32 = jnp.float32
VMEM = pl.BlockSpec(memory_space=pltpu.VMEM)
PARAMS = pltpu.CompilerParams(vmem_limit_bytes=12 * 1024 * 1024)


def move(value, axis, target):
    size, stride = AXES[axis]
    pairs = []
    for i in range(FSDP):
        place = (i // stride) % size
        pairs.append((i, i + (target(place) - place) * stride))
    return lax.ppermute(value, "fsdp", pairs)


def up_y(value):
    return move(value, "y", lambda p: (p + 1) % 4)


def down_y(value):
    return move(value, "y", lambda p: (p + 3) % 4)


def swap_z(value):
    return move(value, "z", lambda p: 1 - p)


def swap_core(value):
    return move(value, "core", lambda p: 1 - p)


def far_x(value):
    return move(value, "x", lambda p: (p + 2) % 4)


def near_x(pair):
    first, second = pair
    return [move(first, "x", lambda p: p ^ 1), move(second, "x", lambda p: 3 - p)]


def swap_replica(value):
    return lax.ppermute(value, "replica", [(0, 1), (1, 0)])


def struct(shape, dtype):
    return jax.ShapeDtypeStruct(shape, dtype)


def weights_kernel(in_ref, down_ref, all_ref, *outs):
    half = all_ref.shape[2]
    whole = [in_ref[0, 0].astype(BF16).T, in_ref[0, 1].astype(BF16).T, down_ref[0].astype(BF16)]
    for k, out_ref in enumerate(outs):
        for i in range(3):
            part = whole[i][k * half : (k + 1) * half]
            out_ref[i] = part
            all_ref[k, i] = part


def own_weights(params_in, params_down):
    depth, width = params_in.shape[2:]
    half = (3, width // 2, depth)
    return pl.pallas_call(
        weights_kernel,
        in_specs=[VMEM] * 2,
        out_specs=[VMEM] * 3,
        out_shape=[struct((2, *half), BF16), struct(half, BF16), struct(half, BF16)],
        cost_estimate=pl.CostEstimate(
            flops=depth * width * 3, bytes_accessed=depth * width * 18, transcendentals=0
        ),
        compiler_params=PARAMS,
        name="own_weights",
    )(params_in, params_down)


def forward_kernel(planes, in_ref, down_ref, *refs):
    count = len(planes)
    pieces, outs = refs[: 2 * count], refs[2 * count :]
    hidden_ref, dgate_ref, dup_ref, rows_ref, cots_ref = outs
    start = 0
    for k, (x_plane, c_plane) in enumerate(planes):
        rows = pieces[2 * k].shape[1]
        rows_ref[start : start + rows] = pieces[2 * k][x_plane]
        cots_ref[start : start + rows] = pieces[2 * k + 1][c_plane]
        start += rows
    width = down_ref.shape[0]
    sides = (((1,), (1,)), ((), ()))
    both = lax.dot_general(in_ref[...], rows_ref[...], sides, preferred_element_type=F32)
    dhidden = lax.dot_general(down_ref[...], cots_ref[...], sides, preferred_element_type=F32)
    gate_pre, up_proj = both[:width], both[width:]
    sig = 1.0 / (1.0 + jnp.exp(-gate_pre))
    silu = gate_pre * sig
    hidden_ref[...] = (silu * up_proj).astype(BF16)
    dgate_ref[...] = (dhidden * up_proj * (sig * (1.0 + gate_pre * (1.0 - sig)))).astype(BF16)
    dup_ref[...] = (dhidden * silu).astype(BF16)


def forward(weights_in, weights_down, pieces):
    width, depth = weights_down.shape
    total = sum(p[0].shape[1] for p in pieces)
    operands = [a for x, _, c, _ in pieces for a in (x, c)]
    return pl.pallas_call(
        functools.partial(forward_kernel, [(p[1], p[3]) for p in pieces]),
        in_specs=[VMEM] * (2 + len(operands)),
        out_specs=[VMEM] * 5,
        out_shape=[struct((width, total), BF16)] * 3 + [struct((total, depth), BF16)] * 2,
        cost_estimate=pl.CostEstimate(
            flops=2 * total * depth * 3 * width,
            bytes_accessed=total * depth * 8 + 6 * width * depth,
            transcendentals=total * width,
        ),
        compiler_params=PARAMS,
        name="forward",
    )(weights_in, weights_down, *operands)


def gradient_kernel(count, start, *refs):
    left, right = refs[:count], refs[count : 2 * count]
    own_ref, near_ref, send_ref, all_ref = refs[2 * count :]
    quarter, depth = own_ref.shape
    row = 0
    for piece in left:
        all_ref[:, row : row + piece.shape[1]] = piece[...]
        row += piece.shape[1]
    tile = 256
    for i in range(depth // tile):
        at = slice(i * tile, (i + 1) * tile)
        here = slice(start + i * tile, start + (i + 1) * tile)
        columns = jnp.concatenate([piece[:, here] for piece in right], axis=0)
        total = jnp.dot(all_ref[...], columns, preferred_element_type=F32)
        own_ref[:, at] = total[:quarter]
        send_ref[0, :, at] = total[quarter : 2 * quarter].astype(BF16)
        near_ref[:, at] = total[2 * quarter : 3 * quarter]
        send_ref[1, :, at] = total[3 * quarter :].astype(BF16)


def gradient(left, right, start, size):
    width = left[0].shape[0]
    rows = sum(r.shape[0] for r in right)
    quarter = width // 4
    return pl.pallas_call(
        functools.partial(gradient_kernel, len(left), start),
        in_specs=[VMEM] * (2 * len(left)),
        out_specs=[VMEM] * 3,
        out_shape=[
            struct((quarter, size), F32),
            struct((quarter, size), F32),
            struct((2, quarter, size), BF16),
        ],
        scratch_shapes=[pltpu.VMEM((width, rows), BF16)],
        cost_estimate=pl.CostEstimate(
            flops=2 * rows * size * width,
            bytes_accessed=rows * size * 2 + rows * width * 2 + width * size * 3,
            transcendentals=0,
        ),
        compiler_params=PARAMS,
        name="gradient",
    )(*left, *right)


def near_sum_kernel(part_ref, core_ref, *outs):
    half = outs[0].shape[0]
    for k, out_ref in enumerate(outs):
        at = slice(k * half, (k + 1) * half)
        out_ref[...] = (part_ref[at] + core_ref[1, at].astype(F32)).astype(BF16)


def near_sum(part, core):
    quarter, size = part.shape
    return pl.pallas_call(
        near_sum_kernel,
        in_specs=[VMEM] * 2,
        out_specs=[VMEM] * 2,
        out_shape=[struct((quarter // 2, size), BF16)] * 2,
        cost_estimate=pl.CostEstimate(
            flops=quarter * size, bytes_accessed=quarter * size * 10, transcendentals=0
        ),
        compiler_params=PARAMS,
        name="near_sum",
    )(part, core)


def adamw(param, grad, first, second):
    first_new = beta_one * first.astype(F32) + (1.0 - beta_one) * grad
    second_new = beta_two * second.astype(F32) + (1.0 - beta_two) * grad * grad
    update = first_new / bias_one / (jnp.sqrt(second_new / bias_two) + epsilon_adam)
    param_new = param - inner_rate * (update + decay_rate * param)
    return (param_new, first_new.astype(BF16), second_new.astype(BF16))


TILE = 512


def inner_kernel(which, start, *refs):
    own, core, near_a, near_b, param, first, second, base = refs[:8]
    first_out, second_out, delta_out = refs[-3:]
    step = pl.program_id(0) * TILE
    part = pl.ds(pl.multiple_of(step, TILE), TILE)
    at = pl.ds(pl.multiple_of(start + step, TILE), TILE)
    near = jnp.concatenate([near_a[:, part].astype(F32), near_b[:, part].astype(F32)], axis=0)
    grad = own[:, part] + core[0, :, part].astype(F32) + near
    if which is None:
        place, shared = (0, slice(None), at), (slice(None), at)
    else:
        grad = grad.T
        place, shared = (0, which, at), (which, at)
    new, first_new, second_new = adamw(param[place], grad, first[place], second[place])
    first_out[...] = first_new.reshape(first_out.shape)
    second_out[...] = second_new.reshape(second_out.shape)
    delta_out[...] = (base[shared] - new).astype(BF16)


def inner_step(sums, param, first, second, base, which=None, start=0, earlier=()):
    own, core, near = sums
    quarter, size = own.shape
    skip = start // TILE
    if which is not None:
        state = pl.BlockSpec((1, 1, TILE, quarter), lambda i: (0, which, i + skip, 0))
        delta = pl.BlockSpec((TILE, quarter), lambda i: (i, 0))
        delta_shape = (size, quarter)
    else:
        state = pl.BlockSpec((1, quarter, TILE), lambda i: (0, 0, i + skip))
        delta = pl.BlockSpec((quarter, TILE), lambda i: (0, i))
        delta_shape = (quarter, size)
    return pl.pallas_call(
        functools.partial(inner_kernel, which, start),
        grid=(size // TILE,),
        in_specs=[VMEM] * 8 + [pl.BlockSpec(memory_space=pl.ANY)] * len(earlier),
        out_specs=[state, state, delta],
        out_shape=[struct(first.shape, BF16), struct(second.shape, BF16), struct(delta_shape, BF16)],
        input_output_aliases={8 + k: k for k in range(len(earlier))},
        cost_estimate=pl.CostEstimate(
            flops=20 * quarter * size, bytes_accessed=26 * quarter * size, transcendentals=quarter * size
        ),
        compiler_params=PARAMS,
        name="inner_step",
    )(own, core, *near, param, first, second, base, *earlier)


def outer_kernel(which, start, *refs):
    own, other, base, outer = refs[:4]
    base_out, outer_out = refs[-2:]
    step = pl.program_id(0) * TILE
    part = pl.ds(pl.multiple_of(step, TILE), TILE)
    at = pl.ds(pl.multiple_of(start + step, TILE), TILE)
    if which is None:
        part, shared = (slice(None), part), (slice(None), at)
    else:
        part, shared = (part,), (which, at)
    grad = (own[part].astype(F32) + other[part].astype(F32)) / 2.0
    new_outer = momentum_keep * outer[shared] + grad
    outer_out[...] = new_outer.reshape(outer_out.shape)
    base_out[...] = (base[shared] - outer_rate * (grad + momentum_keep * new_outer)).reshape(base_out.shape)


def outer_step(own, other, base, outer, which=None, start=0, earlier=()):
    skip = start // TILE
    if which is not None:
        size, quarter = own.shape
        shared = pl.BlockSpec((1, TILE, quarter), lambda i: (which, i + skip, 0))
    else:
        quarter, size = own.shape
        shared = pl.BlockSpec((quarter, TILE), lambda i: (0, i + skip))
    return pl.pallas_call(
        functools.partial(outer_kernel, which, start),
        grid=(size // TILE,),
        in_specs=[VMEM] * 4 + [pl.BlockSpec(memory_space=pl.ANY)] * len(earlier),
        out_specs=[shared, shared],
        out_shape=[struct(base.shape, F32), struct(outer.shape, F32)],
        input_output_aliases={4 + k: k for k in range(len(earlier))},
        cost_estimate=pl.CostEstimate(
            flops=8 * quarter * size, bytes_accessed=20 * quarter * size, transcendentals=0
        ),
        compiler_params=PARAMS,
        name="outer_step",
    )(own, other, base, outer, *earlier)


def after(value, *others):
    return lax.optimization_barrier((value, others))[0]


def local(
    inputs,
    cotangent,
    params_in,
    params_down,
    first_in,
    first_down,
    second_in,
    second_down,
    base_in,
    base_down,
    outer_in,
    outer_down,
):
    own = jnp.concatenate([inputs, cotangent])
    low, high = up_y(own), down_y(own)
    by_x, by_z = far_x(own), swap_z(own)
    mine, *halves = own_weights(params_in, params_down)
    core = swap_core(mine)
    by_xz = swap_z(after(by_x, by_z))
    far = up_y(low)
    near = jnp.stack(near_x(after(halves, by_x)))
    both = swap_core(near)
    low_x, high_x = far_x(after(low, near)), down_y(after(by_x, high))
    beside_z = swap_z(after(jnp.concatenate([low, high]), by_xz))
    low_xz, high_xz = up_y(after(by_xz, far, core)), down_y(after(by_xz, high_x, core))
    far_of_x = far_x(after(far, low_x))
    far_xz_x, far_xz_c = up_y(after(low_xz[:1], both)), down_y(after(high_xz[1:], both))
    far_z_x, far_z_c = up_y(beside_z[:1]), down_y(beside_z[3:])

    parts = [half for quarter in (mine, core, near, both) for half in quarter]
    weights_in = jnp.concatenate([w[k] for k in range(2) for w in parts])
    weights_down = jnp.concatenate([w[2] for w in parts])

    def full(piece):
        return (piece, 0, piece, 1)

    groups = [
        [full(own), full(low), full(high), full(far)],
        [full(by_x), full(low_x), full(high_x), full(far_of_x)],
        [full(by_z), full(by_xz), (beside_z, 0, beside_z, 1), (beside_z, 2, beside_z, 3)],
        [full(low_xz), full(high_xz), (far_xz_x, 0, far_xz_c, 0), (far_z_x, 0, far_z_c, 0)],
    ]
    results = [forward(weights_in, weights_down, group) for group in groups]
    hidden, dgate, dup, rows, cots = [list(r) for r in zip(*results)]

    depth = inputs.shape[2]
    states = (
        (params_down, first_down, second_down, base_down, outer_down),
        (params_in, first_in, second_in, base_in, outer_in),
    )
    steps = (
        (dgate, rows, 1, 0, 0, depth),
        (dup, rows, 1, 1, 0, depth),
        (hidden, cots, 0, None, 0, depth),
    )
    moments, sums, deltas, others, news = [(), ()], [], [], [], [(), ()]
    cores, nears = [], []
    for k, (left, right, array, which, start, size) in enumerate(steps):
        if k >= 2:
            left = after(left, cores[k - 2])
        own_part, near_part, send = gradient(left, right, start, size)
        core_part = swap_core(send)
        cores.append(core_part)
        near_parts = near_sum(near_part, core_part)
        nears.append(near_parts)
        sums.append(near_x(near_parts))
        param, first, second, base, _ = states[array]
        *moments[array], delta = inner_step(
            (own_part, core_part, sums[k]), param, first, second, base, which, start, moments[array]
        )
        deltas.append(delta)
        others.append(swap_replica(delta))
    for k, (_, _, array, which, start, _) in enumerate(steps):
        base, outer = states[array][3:]
        news[array] = outer_step(deltas[k], others[k], base, outer, which, start, news[array])
    (new_base_down, new_outer_down), (new_base_in, new_outer_in) = news
    (fdown, sdown), (fin, sin) = moments
    return (new_base_in, new_base_down, new_outer_in, new_outer_down, fin, fdown, sin, sdown)


def solution(mesh):
    in_specs = (
        P("replica", "fsdp", None),
        P("replica", "fsdp", None),
        P("replica", None, None, "fsdp"),
        P("replica", "fsdp", None),
        P("replica", None, None, "fsdp"),
        P("replica", "fsdp", None),
        P("replica", None, None, "fsdp"),
        P("replica", "fsdp", None),
        P(None, None, "fsdp"),
        P("fsdp", None),
        P(None, None, "fsdp"),
        P("fsdp", None),
    )
    out_specs = (
        P(None, None, "fsdp"),
        P("fsdp", None),
        P(None, None, "fsdp"),
        P("fsdp", None),
        P("replica", None, None, "fsdp"),
        P("replica", "fsdp", None),
        P("replica", None, None, "fsdp"),
        P("replica", "fsdp", None),
    )
    return jax.shard_map(local, mesh=mesh, in_specs=in_specs, out_specs=out_specs, check_vma=False)
```

```python
import functools

import jax
import jax.numpy as jnp
from jax import lax
from jax.experimental import pallas as pl
from jax.experimental.pallas import tpu as pltpu
from jax.sharding import PartitionSpec as P

beta_one = 0.9
beta_two = 0.95
bias_one = 1.0 - 0.9**64
bias_two = 1.0 - 0.95**64
inner_rate = 0.004
decay_rate = 0.1
epsilon_adam = 1e-08
momentum_keep = 0.9
outer_rate = 0.7

AXES = {"x": (4, 16), "z": (2, 8), "y": (4, 2), "core": (2, 1)}
FSDP = 64
BF16 = jnp.bfloat16
F32 = jnp.float32
VMEM = pl.BlockSpec(memory_space=pltpu.VMEM)
PARAMS = pltpu.CompilerParams(vmem_limit_bytes=12 * 1024 * 1024)


def move(value, axis, target):
    size, stride = AXES[axis]
    pairs = []
    for i in range(FSDP):
        place = (i // stride) % size
        pairs.append((i, i + (target(place) - place) * stride))
    return lax.ppermute(value, "fsdp", pairs)


def up_y(value):
    return move(value, "y", lambda p: (p + 1) % 4)


def down_y(value):
    return move(value, "y", lambda p: (p + 3) % 4)


def swap_z(value):
    return move(value, "z", lambda p: 1 - p)


def swap_core(value):
    return move(value, "core", lambda p: 1 - p)


def both_cores(value):
    pairs = [[i, i + 1] for i in range(0, FSDP, 2)]
    return lax.all_gather(value, "fsdp", axis_index_groups=pairs)


def far_x(value):
    return move(value, "x", lambda p: (p + 2) % 4)


def near_x(pair):
    first, second = pair
    return [move(first, "x", lambda p: p ^ 1), move(second, "x", lambda p: 3 - p)]


def swap_replica(value):
    return lax.ppermute(value, "replica", [(0, 1), (1, 0)])


def struct(shape, dtype):
    return jax.ShapeDtypeStruct(shape, dtype)


def weights_kernel(in_ref, down_ref, all_ref, *outs):
    half = all_ref.shape[2]
    whole = [in_ref[0, 0].astype(BF16).T, in_ref[0, 1].astype(BF16).T, down_ref[0].astype(BF16)]
    for k, out_ref in enumerate(outs):
        for i in range(3):
            part = whole[i][k * half : (k + 1) * half]
            out_ref[i] = part
            all_ref[k, i] = part


def own_weights(params_in, params_down):
    depth, width = params_in.shape[2:]
    half = (3, width // 2, depth)
    return pl.pallas_call(
        weights_kernel,
        in_specs=[VMEM] * 2,
        out_specs=[VMEM] * 3,
        out_shape=[struct((2, *half), BF16), struct(half, BF16), struct(half, BF16)],
        cost_estimate=pl.CostEstimate(
            flops=depth * width * 3, bytes_accessed=depth * width * 18, transcendentals=0
        ),
        compiler_params=PARAMS,
        name="own_weights",
    )(params_in, params_down)


def all_weights_kernel(*refs):
    parts, (in_ref, down_ref) = refs[:8], refs[8:]
    cores, mine, near, both = parts[:2], parts[2:4], parts[4:6], parts[6:]
    half = mine[0].shape[1]
    width = down_ref.shape[0]
    for i in range(3):
        pieces = [ref[i] for ref in mine] + [ref[i] for ref in cores]
        pieces += [ref[i] for ref in (*near, *both)]
        for k, piece in enumerate(pieces):
            if i < 2:
                in_ref[i * width + k * half : i * width + (k + 1) * half] = piece
            else:
                down_ref[k * half : (k + 1) * half] = piece


def all_weights(cores, mine, near, both):
    half, depth = mine[0].shape[1:]
    return pl.pallas_call(
        all_weights_kernel,
        in_specs=[VMEM] * 8,
        out_specs=[VMEM] * 2,
        out_shape=[struct((16 * half, depth), BF16), struct((8 * half, depth), BF16)],
        cost_estimate=pl.CostEstimate(
            flops=0, bytes_accessed=8 * half * depth * 12, transcendentals=0
        ),
        compiler_params=PARAMS,
        name="all_weights",
    )(*cores, *mine, *near, *both)


def forward_kernel(planes, in_ref, down_ref, *refs):
    count = len(planes)
    pieces, outs = refs[: 2 * count], refs[2 * count :]
    hidden_ref, dgate_ref, dup_ref, rows_ref, cots_ref = outs
    start = 0
    for k, (x_plane, c_plane) in enumerate(planes):
        rows = pieces[2 * k].shape[1]
        rows_ref[start : start + rows] = pieces[2 * k][x_plane]
        cots_ref[start : start + rows] = pieces[2 * k + 1][c_plane]
        start += rows
    width = down_ref.shape[0]
    sides = (((1,), (1,)), ((), ()))
    both = lax.dot_general(in_ref[...], rows_ref[...], sides, preferred_element_type=F32)
    dhidden = lax.dot_general(down_ref[...], cots_ref[...], sides, preferred_element_type=F32)
    gate_pre, up_proj = both[:width], both[width:]
    sig = 1.0 / (1.0 + jnp.exp(-gate_pre))
    silu = gate_pre * sig
    hidden_ref[...] = (silu * up_proj).astype(BF16)
    dgate_ref[...] = (dhidden * up_proj * (sig * (1.0 + gate_pre * (1.0 - sig)))).astype(BF16)
    dup_ref[...] = (dhidden * silu).astype(BF16)


def forward(weights_in, weights_down, pieces):
    width, depth = weights_down.shape
    total = sum(p[0].shape[1] for p in pieces)
    operands = [a for x, _, c, _ in pieces for a in (x, c)]
    return pl.pallas_call(
        functools.partial(forward_kernel, [(p[1], p[3]) for p in pieces]),
        in_specs=[VMEM] * (2 + len(operands)),
        out_specs=[VMEM] * 5,
        out_shape=[struct((width, total), BF16)] * 3 + [struct((total, depth), BF16)] * 2,
        cost_estimate=pl.CostEstimate(
            flops=2 * total * depth * 3 * width,
            bytes_accessed=total * depth * 8 + 6 * width * depth,
            transcendentals=total * width,
        ),
        compiler_params=PARAMS,
        name="forward",
    )(weights_in, weights_down, *operands)


def gradient_kernel(count, start, *refs):
    left, right = refs[:count], refs[count : 2 * count]
    own_ref, near_ref, send_ref, all_ref = refs[2 * count :]
    quarter, depth = own_ref.shape
    row = 0
    for piece in left:
        all_ref[:, row : row + piece.shape[1]] = piece[...]
        row += piece.shape[1]
    tile = 256
    for i in range(depth // tile):
        at = slice(i * tile, (i + 1) * tile)
        here = slice(start + i * tile, start + (i + 1) * tile)
        columns = jnp.concatenate([piece[:, here] for piece in right], axis=0)
        total = jnp.dot(all_ref[...], columns, preferred_element_type=F32)
        own_ref[:, at] = total[:quarter]
        send_ref[0, :, at] = total[quarter : 2 * quarter].astype(BF16)
        near_ref[:, at] = total[2 * quarter : 3 * quarter]
        send_ref[1, :, at] = total[3 * quarter :].astype(BF16)


def gradient(left, right, start, size):
    width = left[0].shape[0]
    rows = sum(r.shape[0] for r in right)
    quarter = width // 4
    return pl.pallas_call(
        functools.partial(gradient_kernel, len(left), start),
        in_specs=[VMEM] * (2 * len(left)),
        out_specs=[VMEM] * 3,
        out_shape=[struct((quarter, size), F32)] * 2 + [struct((2, quarter, size), BF16)],
        scratch_shapes=[pltpu.VMEM((width, rows), BF16)],
        cost_estimate=pl.CostEstimate(
            flops=2 * rows * size * width,
            bytes_accessed=rows * size * 2 + rows * width * 2 + width * size * 3,
            transcendentals=0,
        ),
        compiler_params=PARAMS,
        name="gradient",
    )(*left, *right)


def near_sum_kernel(part_ref, core_ref, *outs):
    half = outs[0].shape[0]
    for k, out_ref in enumerate(outs):
        at = slice(k * half, (k + 1) * half)
        out_ref[...] = (part_ref[at] + core_ref[1, at].astype(F32)).astype(BF16)


def near_sum(part, core):
    quarter, size = part.shape
    return pl.pallas_call(
        near_sum_kernel,
        in_specs=[VMEM] * 2,
        out_specs=[VMEM] * 2,
        out_shape=[struct((quarter // 2, size), BF16)] * 2,
        cost_estimate=pl.CostEstimate(
            flops=quarter * size, bytes_accessed=quarter * size * 10, transcendentals=0
        ),
        compiler_params=PARAMS,
        name="near_sum",
    )(part, core)


def adamw(param, grad, first, second):
    first_new = beta_one * first.astype(F32) + (1.0 - beta_one) * grad
    second_new = beta_two * second.astype(F32) + (1.0 - beta_two) * grad * grad
    update = first_new / bias_one / (jnp.sqrt(second_new / bias_two) + epsilon_adam)
    param_new = param - inner_rate * (update + decay_rate * param)
    return (param_new, first_new.astype(BF16), second_new.astype(BF16))


TILE = 1024


def inner_kernel(which, start, *refs):
    own, core, near_a, near_b, param, first, second, base = refs[:8]
    first_out, second_out, delta_out = refs[-3:]
    step = pl.program_id(0) * TILE
    part = pl.ds(pl.multiple_of(step, TILE), TILE)
    at = pl.ds(pl.multiple_of(start + step, TILE), TILE)
    near = jnp.concatenate([near_a[:, part].astype(F32), near_b[:, part].astype(F32)], axis=0)
    grad = own[:, part] + core[0, :, part].astype(F32) + near
    if which is None:
        place, shared = (0, slice(None), at), (slice(None), at)
    else:
        grad = grad.T
        place, shared = (0, which, at), (which, at)
    new, first_new, second_new = adamw(param[place], grad, first[place], second[place])
    first_out[...] = first_new.reshape(first_out.shape)
    second_out[...] = second_new.reshape(second_out.shape)
    delta_out[...] = (base[shared] - new).astype(BF16)


def inner_step(sums, param, first, second, base, which=None, start=0, earlier=()):
    own, core, near = sums
    quarter, size = own.shape
    skip = start // TILE
    if which is not None:
        state = pl.BlockSpec((1, 1, TILE, quarter), lambda i: (0, which, i + skip, 0))
        delta = pl.BlockSpec((TILE, quarter), lambda i: (i, 0))
        delta_shape = (size, quarter)
    else:
        state = pl.BlockSpec((1, quarter, TILE), lambda i: (0, 0, i + skip))
        delta = pl.BlockSpec((quarter, TILE), lambda i: (0, i))
        delta_shape = (quarter, size)
    return pl.pallas_call(
        functools.partial(inner_kernel, which, start),
        grid=(size // TILE,),
        in_specs=[VMEM] * 8 + [pl.BlockSpec(memory_space=pl.ANY)] * len(earlier),
        out_specs=[state, state, delta],
        out_shape=[struct(first.shape, BF16), struct(second.shape, BF16), struct(delta_shape, BF16)],
        input_output_aliases={8 + k: k for k in range(len(earlier))},
        cost_estimate=pl.CostEstimate(
            flops=20 * quarter * size, bytes_accessed=26 * quarter * size, transcendentals=quarter * size
        ),
        compiler_params=PARAMS,
        name="inner_step",
    )(own, core, *near, param, first, second, base, *earlier)


def outer_kernel(which, start, *refs):
    own, other, base, outer = refs[:4]
    base_out, outer_out = refs[-2:]
    step = pl.program_id(0) * TILE
    part = pl.ds(pl.multiple_of(step, TILE), TILE)
    at = pl.ds(pl.multiple_of(start + step, TILE), TILE)
    if which is None:
        part, shared = (slice(None), part), (slice(None), at)
    else:
        part, shared = (part,), (which, at)
    grad = (own[part].astype(F32) + other[part].astype(F32)) / 2.0
    new_outer = momentum_keep * outer[shared] + grad
    outer_out[...] = new_outer.reshape(outer_out.shape)
    base_out[...] = (base[shared] - outer_rate * (grad + momentum_keep * new_outer)).reshape(base_out.shape)


def outer_step(own, other, base, outer, which=None, start=0, earlier=()):
    skip = start // TILE
    if which is not None:
        size, quarter = own.shape
        shared = pl.BlockSpec((1, TILE, quarter), lambda i: (which, i + skip, 0))
    else:
        quarter, size = own.shape
        shared = pl.BlockSpec((quarter, TILE), lambda i: (0, i + skip))
    return pl.pallas_call(
        functools.partial(outer_kernel, which, start),
        grid=(size // TILE,),
        in_specs=[VMEM] * 4 + [pl.BlockSpec(memory_space=pl.ANY)] * len(earlier),
        out_specs=[shared, shared],
        out_shape=[struct(base.shape, F32), struct(outer.shape, F32)],
        input_output_aliases={4 + k: k for k in range(len(earlier))},
        cost_estimate=pl.CostEstimate(
            flops=8 * quarter * size, bytes_accessed=20 * quarter * size, transcendentals=0
        ),
        compiler_params=PARAMS,
        name="outer_step",
    )(own, other, base, outer, *earlier)


def after(value, *others):
    return lax.optimization_barrier((value, others))[0]


def local(
    inputs,
    cotangent,
    params_in,
    params_down,
    first_in,
    first_down,
    second_in,
    second_down,
    base_in,
    base_down,
    outer_in,
    outer_down,
):
    own = jnp.concatenate([inputs, cotangent])
    low, high = up_y(own), down_y(own)
    by_x, by_z = far_x(own), swap_z(own)
    mine, *halves = own_weights(params_in, params_down)
    cores = [swap_core(w) for w in halves]
    by_xz = swap_z(after(by_x, by_z))
    far = up_y(low)
    near = near_x(after(halves, by_x))
    both = [swap_core(w) for w in near]
    low_x, high_x = far_x(after(low, near)), down_y(after(by_x, high))
    beside_z = swap_z(after(jnp.concatenate([low, high]), by_xz))
    low_xz, high_xz = up_y(after(by_xz, far)), down_y(after(by_xz, high_x))
    far_of_x = far_x(after(far, low_x))
    far_xz_x, far_xz_c = up_y(low_xz[:1]), down_y(high_xz[1:])
    far_z_x, far_z_c = up_y(beside_z[:1]), down_y(beside_z[3:])

    weights_in, weights_down = all_weights(cores, halves, near, both)

    def full(piece):
        return (piece, 0, piece, 1)

    groups = [
        [full(own), full(low), full(high), full(far)],
        [full(by_x), full(low_x), full(high_x), full(low_xz)],
        [full(by_z), full(by_xz), (beside_z, 0, beside_z, 1), (beside_z, 2, beside_z, 3)],
        [full(far_of_x), full(high_xz), (far_xz_x, 0, far_xz_c, 0), (far_z_x, 0, far_z_c, 0)],
    ]
    results = [forward(weights_in, weights_down, group) for group in groups]
    hidden, dgate, dup, rows, cots = [list(r) for r in zip(*results)]

    depth = inputs.shape[2]
    states = (
        (params_down, first_down, second_down, base_down, outer_down),
        (params_in, first_in, second_in, base_in, outer_in),
    )
    steps = (
        (dgate, rows, 1, 0, 0, depth),
        (dup, rows, 1, 1, 0, depth),
        (hidden, cots, 0, None, 0, depth),
    )
    moments, sums, deltas, others, news = [(), ()], [], [], [], [(), ()]
    cores, nears = [], []
    for k, (left, right, array, which, start, size) in enumerate(steps):
        if k >= 2:
            left = after(left, cores[k - 2])
        own_part, near_part, send = gradient(left, right, start, size)
        core_part = swap_core(send)
        cores.append(core_part)
        near_parts = near_sum(near_part, core_part)
        nears.append(near_parts)
        sums.append(near_x(near_parts))
        param, first, second, base, _ = states[array]
        *moments[array], delta = inner_step(
            (own_part, core_part, sums[k]), param, first, second, base, which, start, moments[array]
        )
        deltas.append(delta)
        others.append(swap_replica(delta))
    for k, (_, _, array, which, start, _) in enumerate(steps):
        base, outer = states[array][3:]
        news[array] = outer_step(deltas[k], others[k], base, outer, which, start, news[array])
    (new_base_down, new_outer_down), (new_base_in, new_outer_in) = news
    (fdown, sdown), (fin, sin) = moments
    return (new_base_in, new_base_down, new_outer_in, new_outer_down, fin, fdown, sin, sdown)


def solution(mesh):
    in_specs = (
        P("replica", "fsdp", None),
        P("replica", "fsdp", None),
        P("replica", None, None, "fsdp"),
        P("replica", "fsdp", None),
        P("replica", None, None, "fsdp"),
        P("replica", "fsdp", None),
        P("replica", None, None, "fsdp"),
        P("replica", "fsdp", None),
        P(None, None, "fsdp"),
        P("fsdp", None),
        P(None, None, "fsdp"),
        P("fsdp", None),
    )
    out_specs = (
        P(None, None, "fsdp"),
        P("fsdp", None),
        P(None, None, "fsdp"),
        P("fsdp", None),
        P("replica", None, None, "fsdp"),
        P("replica", "fsdp", None),
        P("replica", None, None, "fsdp"),
        P("replica", "fsdp", None),
    )
    return jax.shard_map(local, mesh=mesh, in_specs=in_specs, out_specs=out_specs, check_vma=False)
```

```python
import functools

import jax
import jax.numpy as jnp
from jax import lax
from jax.experimental import pallas as pl
from jax.experimental.pallas import tpu as pltpu
from jax.sharding import PartitionSpec as P

beta_one = 0.9
beta_two = 0.95
bias_one = 1.0 - 0.9**64
bias_two = 1.0 - 0.95**64
inner_rate = 0.004
decay_rate = 0.1
epsilon_adam = 1e-08
momentum_keep = 0.9
outer_rate = 0.7

AXES = {"x": (4, 16), "z": (2, 8), "y": (4, 2), "core": (2, 1)}
FSDP = 64
BF16 = jnp.bfloat16
F32 = jnp.float32
VMEM = pl.BlockSpec(memory_space=pltpu.VMEM)
PARAMS = pltpu.CompilerParams(vmem_limit_bytes=12 * 1024 * 1024)


def move(value, axis, target):
    size, stride = AXES[axis]
    pairs = []
    for i in range(FSDP):
        place = (i // stride) % size
        pairs.append((i, i + (target(place) - place) * stride))
    return lax.ppermute(value, "fsdp", pairs)


def up_y(value):
    return move(value, "y", lambda p: (p + 1) % 4)


def down_y(value):
    return move(value, "y", lambda p: (p + 3) % 4)


def swap_z(value):
    return move(value, "z", lambda p: 1 - p)


def swap_core(value):
    return move(value, "core", lambda p: 1 - p)


def both_cores(value):
    pairs = [[i, i + 1] for i in range(0, FSDP, 2)]
    return lax.all_gather(value, "fsdp", axis_index_groups=pairs)


def far_x(value):
    return move(value, "x", lambda p: (p + 2) % 4)


def near_x(pair):
    first, second = pair
    return [move(first, "x", lambda p: p ^ 1), move(second, "x", lambda p: 3 - p)]


def swap_replica(value):
    return lax.ppermute(value, "replica", [(0, 1), (1, 0)])


def struct(shape, dtype):
    return jax.ShapeDtypeStruct(shape, dtype)


def own_rows_kernel(in_ref, cot_ref, out_ref, sems):
    copies = [
        pltpu.make_async_copy(ref, out_ref.at[k : k + 1], sems.at[k])
        for k, ref in enumerate((in_ref, cot_ref))
    ]
    for copy in copies:
        copy.start()
    for copy in copies:
        copy.wait()


def own_rows(inputs, cotangent):
    rows, depth = inputs.shape[1:]
    return pl.pallas_call(
        own_rows_kernel,
        in_specs=[pl.BlockSpec(memory_space=pl.ANY)] * 2,
        out_specs=VMEM,
        out_shape=struct((2, rows, depth), BF16),
        scratch_shapes=[pltpu.SemaphoreType.DMA((2,))],
        cost_estimate=pl.CostEstimate(flops=0, bytes_accessed=rows * depth * 8, transcendentals=0),
        compiler_params=pltpu.CompilerParams(vmem_limit_bytes=56 * 1024 * 1024),
        name="own_rows",
    )(inputs, cotangent)


def weights_kernel(in_ref, down_ref, all_ref, *outs):
    half = all_ref.shape[2]
    whole = [in_ref[0, 0].astype(BF16).T, in_ref[0, 1].astype(BF16).T, down_ref[0].astype(BF16)]
    for k, out_ref in enumerate(outs):
        for i in range(3):
            part = whole[i][k * half : (k + 1) * half]
            out_ref[i] = part
            all_ref[k, i] = part


def own_weights(params_in, params_down):
    depth, width = params_in.shape[2:]
    half = (3, width // 2, depth)
    return pl.pallas_call(
        weights_kernel,
        in_specs=[VMEM] * 2,
        out_specs=[VMEM] * 3,
        out_shape=[struct((2, *half), BF16), struct(half, BF16), struct(half, BF16)],
        cost_estimate=pl.CostEstimate(
            flops=depth * width * 3, bytes_accessed=depth * width * 18, transcendentals=0
        ),
        compiler_params=PARAMS,
        name="own_weights",
    )(params_in, params_down)


def all_weights_kernel(*refs):
    parts, (in_ref, down_ref) = refs[:8], refs[8:]
    cores, mine, near, both = parts[:2], parts[2:4], parts[4:6], parts[6:]
    half = mine[0].shape[1]
    width = down_ref.shape[0]
    for i in range(3):
        pieces = [ref[i] for ref in mine] + [ref[i] for ref in cores]
        pieces += [ref[i] for ref in (*near, *both)]
        for k, piece in enumerate(pieces):
            if i < 2:
                in_ref[i * width + k * half : i * width + (k + 1) * half] = piece
            else:
                down_ref[k * half : (k + 1) * half] = piece


def all_weights(cores, mine, near, both):
    half, depth = mine[0].shape[1:]
    return pl.pallas_call(
        all_weights_kernel,
        in_specs=[VMEM] * 8,
        out_specs=[VMEM] * 2,
        out_shape=[struct((16 * half, depth), BF16), struct((8 * half, depth), BF16)],
        cost_estimate=pl.CostEstimate(
            flops=0, bytes_accessed=8 * half * depth * 12, transcendentals=0
        ),
        compiler_params=PARAMS,
        name="all_weights",
    )(*cores, *mine, *near, *both)


def forward_kernel(planes, in_ref, down_ref, *refs):
    count = len(planes)
    pieces, outs = refs[: 2 * count], refs[2 * count :]
    hidden_ref, dgate_ref, dup_ref, rows_ref, cots_ref = outs
    start = 0
    for k, (x_plane, c_plane) in enumerate(planes):
        rows = pieces[2 * k].shape[1]
        rows_ref[start : start + rows] = pieces[2 * k][x_plane]
        cots_ref[start : start + rows] = pieces[2 * k + 1][c_plane]
        start += rows
    width = down_ref.shape[0]
    sides = (((1,), (1,)), ((), ()))
    both = lax.dot_general(in_ref[...], rows_ref[...], sides, preferred_element_type=F32)
    dhidden = lax.dot_general(down_ref[...], cots_ref[...], sides, preferred_element_type=F32)
    gate_pre, up_proj = both[:width], both[width:]
    sig = 1.0 / (1.0 + jnp.exp(-gate_pre))
    silu = gate_pre * sig
    hidden_ref[...] = (silu * up_proj).astype(BF16)
    dgate_ref[...] = (dhidden * up_proj * (sig * (1.0 + gate_pre * (1.0 - sig)))).astype(BF16)
    dup_ref[...] = (dhidden * silu).astype(BF16)


def forward(weights_in, weights_down, pieces):
    width, depth = weights_down.shape
    total = sum(p[0].shape[1] for p in pieces)
    operands = [a for x, _, c, _ in pieces for a in (x, c)]
    return pl.pallas_call(
        functools.partial(forward_kernel, [(p[1], p[3]) for p in pieces]),
        in_specs=[VMEM] * (2 + len(operands)),
        out_specs=[VMEM] * 5,
        out_shape=[struct((width, total), BF16)] * 3 + [struct((total, depth), BF16)] * 2,
        cost_estimate=pl.CostEstimate(
            flops=2 * total * depth * 3 * width,
            bytes_accessed=total * depth * 8 + 6 * width * depth,
            transcendentals=total * width,
        ),
        compiler_params=PARAMS,
        name="forward",
    )(weights_in, weights_down, *operands)


def gradient_kernel(count, start, *refs):
    left, right = refs[:count], refs[count : 2 * count]
    own_ref, near_ref, send_ref, all_ref = refs[2 * count :]
    quarter, depth = own_ref.shape
    row = 0
    for piece in left:
        all_ref[:, row : row + piece.shape[1]] = piece[...]
        row += piece.shape[1]
    tile = 256
    for i in range(depth // tile):
        at = slice(i * tile, (i + 1) * tile)
        here = slice(start + i * tile, start + (i + 1) * tile)
        columns = jnp.concatenate([piece[:, here] for piece in right], axis=0)
        total = jnp.dot(all_ref[...], columns, preferred_element_type=F32)
        own_ref[:, at] = total[:quarter]
        send_ref[0, :, at] = total[quarter : 2 * quarter].astype(BF16)
        near_ref[:, at] = total[2 * quarter : 3 * quarter]
        send_ref[1, :, at] = total[3 * quarter :].astype(BF16)


def gradient(left, right, start, size):
    width = left[0].shape[0]
    rows = sum(r.shape[0] for r in right)
    quarter = width // 4
    return pl.pallas_call(
        functools.partial(gradient_kernel, len(left), start),
        in_specs=[VMEM] * (2 * len(left)),
        out_specs=[VMEM] * 3,
        out_shape=[struct((quarter, size), F32)] * 2 + [struct((2, quarter, size), BF16)],
        scratch_shapes=[pltpu.VMEM((width, rows), BF16)],
        cost_estimate=pl.CostEstimate(
            flops=2 * rows * size * width,
            bytes_accessed=rows * size * 2 + rows * width * 2 + width * size * 3,
            transcendentals=0,
        ),
        compiler_params=PARAMS,
        name="gradient",
    )(*left, *right)


def near_sum_kernel(part_ref, core_ref, *outs):
    half = outs[0].shape[0]
    for k, out_ref in enumerate(outs):
        at = slice(k * half, (k + 1) * half)
        out_ref[...] = (part_ref[at] + core_ref[1, at].astype(F32)).astype(BF16)


def near_sum(part, core):
    quarter, size = part.shape
    return pl.pallas_call(
        near_sum_kernel,
        in_specs=[VMEM] * 2,
        out_specs=[VMEM] * 2,
        out_shape=[struct((quarter // 2, size), BF16)] * 2,
        cost_estimate=pl.CostEstimate(
            flops=quarter * size, bytes_accessed=quarter * size * 10, transcendentals=0
        ),
        compiler_params=PARAMS,
        name="near_sum",
    )(part, core)


def adamw(param, grad, first, second):
    first_new = beta_one * first.astype(F32) + (1.0 - beta_one) * grad
    second_new = beta_two * second.astype(F32) + (1.0 - beta_two) * grad * grad
    update = first_new / bias_one / (jnp.sqrt(second_new / bias_two) + epsilon_adam)
    param_new = param - inner_rate * (update + decay_rate * param)
    return (param_new, first_new.astype(BF16), second_new.astype(BF16))


TILE = 1024


def inner_kernel(which, start, *refs):
    own, core, near_a, near_b, param, first, second, base = refs[:8]
    first_out, second_out, delta_out = refs[-3:]
    step = pl.program_id(0) * TILE
    part = pl.ds(pl.multiple_of(step, TILE), TILE)
    at = pl.ds(pl.multiple_of(start + step, TILE), TILE)
    near = jnp.concatenate([near_a[:, part].astype(F32), near_b[:, part].astype(F32)], axis=0)
    grad = own[:, part] + core[0, :, part].astype(F32) + near
    if which is None:
        place, shared = (0, slice(None), at), (slice(None), at)
    else:
        grad = grad.T
        place, shared = (0, which, at), (which, at)
    new, first_new, second_new = adamw(param[place], grad, first[place], second[place])
    first_out[...] = first_new.reshape(first_out.shape)
    second_out[...] = second_new.reshape(second_out.shape)
    delta_out[...] = (base[shared] - new).astype(BF16)


def inner_step(sums, param, first, second, base, which=None, start=0, earlier=()):
    own, core, near = sums
    quarter, size = own.shape
    skip = start // TILE
    if which is not None:
        state = pl.BlockSpec((1, 1, TILE, quarter), lambda i: (0, which, i + skip, 0))
        delta = pl.BlockSpec((TILE, quarter), lambda i: (i, 0))
        delta_shape = (size, quarter)
    else:
        state = pl.BlockSpec((1, quarter, TILE), lambda i: (0, 0, i + skip))
        delta = pl.BlockSpec((quarter, TILE), lambda i: (0, i))
        delta_shape = (quarter, size)
    return pl.pallas_call(
        functools.partial(inner_kernel, which, start),
        grid=(size // TILE,),
        in_specs=[VMEM] * 8 + [pl.BlockSpec(memory_space=pl.ANY)] * len(earlier),
        out_specs=[state, state, delta],
        out_shape=[struct(first.shape, BF16), struct(second.shape, BF16), struct(delta_shape, BF16)],
        input_output_aliases={8 + k: k for k in range(len(earlier))},
        cost_estimate=pl.CostEstimate(
            flops=20 * quarter * size, bytes_accessed=26 * quarter * size, transcendentals=quarter * size
        ),
        compiler_params=PARAMS,
        name="inner_step",
    )(own, core, *near, param, first, second, base, *earlier)


def outer_kernel(which, start, *refs):
    own, other, base, outer = refs[:4]
    base_out, outer_out = refs[-2:]
    step = pl.program_id(0) * TILE
    part = pl.ds(pl.multiple_of(step, TILE), TILE)
    at = pl.ds(pl.multiple_of(start + step, TILE), TILE)
    if which is None:
        part, shared = (slice(None), part), (slice(None), at)
    else:
        part, shared = (part,), (which, at)
    grad = (own[part].astype(F32) + other[part].astype(F32)) / 2.0
    new_outer = momentum_keep * outer[shared] + grad
    outer_out[...] = new_outer.reshape(outer_out.shape)
    base_out[...] = (base[shared] - outer_rate * (grad + momentum_keep * new_outer)).reshape(base_out.shape)


def outer_step(own, other, base, outer, which=None, start=0, earlier=()):
    skip = start // TILE
    if which is not None:
        size, quarter = own.shape
        shared = pl.BlockSpec((1, TILE, quarter), lambda i: (which, i + skip, 0))
    else:
        quarter, size = own.shape
        shared = pl.BlockSpec((quarter, TILE), lambda i: (0, i + skip))
    return pl.pallas_call(
        functools.partial(outer_kernel, which, start),
        grid=(size // TILE,),
        in_specs=[VMEM] * 4 + [pl.BlockSpec(memory_space=pl.ANY)] * len(earlier),
        out_specs=[shared, shared],
        out_shape=[struct(base.shape, F32), struct(outer.shape, F32)],
        input_output_aliases={4 + k: k for k in range(len(earlier))},
        cost_estimate=pl.CostEstimate(
            flops=8 * quarter * size, bytes_accessed=20 * quarter * size, transcendentals=0
        ),
        compiler_params=PARAMS,
        name="outer_step",
    )(own, other, base, outer, *earlier)


def after(value, *others):
    return lax.optimization_barrier((value, others))[0]


def local(
    inputs,
    cotangent,
    params_in,
    params_down,
    first_in,
    first_down,
    second_in,
    second_down,
    base_in,
    base_down,
    outer_in,
    outer_down,
):
    own = own_rows(inputs, cotangent)
    low, high = up_y(own), down_y(own)
    by_x, by_z = far_x(own), swap_z(own)
    mine, *halves = own_weights(params_in, params_down)
    cores = [swap_core(w) for w in halves]
    by_xz = swap_z(after(by_x, by_z))
    far = up_y(low)
    near = near_x(after(halves, by_x))
    both = [swap_core(w) for w in near]
    low_x, high_x = far_x(after(low, near)), down_y(after(by_x, high))
    beside_z = swap_z(after(jnp.concatenate([low, high]), by_xz))
    low_xz, high_xz = up_y(after(by_xz, far)), down_y(after(by_xz, high_x))
    far_of_x = far_x(after(far, low_x))
    far_xz_x, far_xz_c = up_y(low_xz[:1]), down_y(high_xz[1:])
    far_z_x, far_z_c = up_y(beside_z[:1]), down_y(beside_z[3:])

    weights_in, weights_down = all_weights(cores, halves, near, both)

    def full(piece):
        return (piece, 0, piece, 1)

    groups = [
        [full(own), full(low), full(high), full(far)],
        [full(by_x), full(low_x), full(high_x), full(low_xz)],
        [full(by_z), full(by_xz), (beside_z, 0, beside_z, 1), (beside_z, 2, beside_z, 3)],
        [full(far_of_x), full(high_xz), (far_xz_x, 0, far_xz_c, 0), (far_z_x, 0, far_z_c, 0)],
    ]
    results = [forward(weights_in, weights_down, group) for group in groups]
    hidden, dgate, dup, rows, cots = [list(r) for r in zip(*results)]

    depth = inputs.shape[2]
    states = (
        (params_down, first_down, second_down, base_down, outer_down),
        (params_in, first_in, second_in, base_in, outer_in),
    )
    steps = (
        (dgate, rows, 1, 0, 0, depth),
        (dup, rows, 1, 1, 0, depth),
        (hidden, cots, 0, None, 0, depth),
    )
    moments, sums, deltas, others, news = [(), ()], [], [], [], [(), ()]
    cores, nears = [], []
    for k, (left, right, array, which, start, size) in enumerate(steps):
        if k >= 2:
            left = after(left, cores[k - 2])
        own_part, near_part, send = gradient(left, right, start, size)
        core_part = swap_core(send)
        cores.append(core_part)
        near_parts = near_sum(near_part, core_part)
        nears.append(near_parts)
        sums.append(near_x(near_parts))
        param, first, second, base, _ = states[array]
        *moments[array], delta = inner_step(
            (own_part, core_part, sums[k]), param, first, second, base, which, start, moments[array]
        )
        deltas.append(delta)
        others.append(swap_replica(delta))
    for k, (_, _, array, which, start, _) in enumerate(steps):
        base, outer = states[array][3:]
        news[array] = outer_step(deltas[k], others[k], base, outer, which, start, news[array])
    (new_base_down, new_outer_down), (new_base_in, new_outer_in) = news
    (fdown, sdown), (fin, sin) = moments
    return (new_base_in, new_base_down, new_outer_in, new_outer_down, fin, fdown, sin, sdown)


def solution(mesh):
    in_specs = (
        P("replica", "fsdp", None),
        P("replica", "fsdp", None),
        P("replica", None, None, "fsdp"),
        P("replica", "fsdp", None),
        P("replica", None, None, "fsdp"),
        P("replica", "fsdp", None),
        P("replica", None, None, "fsdp"),
        P("replica", "fsdp", None),
        P(None, None, "fsdp"),
        P("fsdp", None),
        P(None, None, "fsdp"),
        P("fsdp", None),
    )
    out_specs = (
        P(None, None, "fsdp"),
        P("fsdp", None),
        P(None, None, "fsdp"),
        P("fsdp", None),
        P("replica", None, None, "fsdp"),
        P("replica", "fsdp", None),
        P("replica", None, None, "fsdp"),
        P("replica", "fsdp", None),
    )
    return jax.shard_map(local, mesh=mesh, in_specs=in_specs, out_specs=out_specs, check_vma=False)
```
